512 devices in a mesh: prow: 16 (over z, core), pcol: 32 (over y, x).
Axes of the slice: x: 4, y: 8, z: 8, core: 2. Of those that a mesh axis runs over, the one named last changes fastest.
Arguments:
- hamiltonian: float32 [16384, 16384], P('prow', 'pcol'), may hold values from -60 to 60, as said below
Outputs:
- reduced: float32 [16384, 16384], P('prow', 'pcol')
The draws below stay inside these ranges and needn't reach their ends.
Inputs may be any that keep to these rules, and one draw needn't show every extreme that they name: hamiltonian holds a symmetric matrix in the stated storage: H[a, b] = H[b, a] exactly.
All inputs are finite; a program needn't handle non-finite values.
Results may differ from the reference program's by a relative error of at most 0.0003.
Values sent between devices are 32-bit elements; how exact they have to be, the bound alone decides.
A program may use at most 64 MiB of HBM per device.

```python
import jax
import jax.numpy as jnp
from jax import lax

NB = 128
ROWS_DEV = 1024
ORDER = 16384
COLS_DEV = 512


def draw_hamiltonian(key, part):
    key = jax.random.fold_in(key, 17)
    keys_all = jax.random.split(key, 4)
    prow_count = ORDER // ROWS_DEV
    pcol_count = ORDER // COLS_DEV
    stored = jnp.arange(ORDER, dtype=jnp.int32)
    row_global = (stored % ROWS_DEV // NB * prow_count + stored // ROWS_DEV) * NB + stored % NB
    col_global = (stored % COLS_DEV // NB * pcol_count + stored // COLS_DEV) * NB + stored % NB
    rising = 1.0 + 2.0 * (stored // NB % prow_count).astype(jnp.float32) / (prow_count - 1)
    noise = jnp.clip(jax.random.normal(keys_all[0], (ORDER, ORDER), jnp.float32), -4.0, 4.0)
    spread = jnp.exp(jax.random.uniform(keys_all[1], (ORDER,), jnp.float32, 0.0, 1.1)) * 0.4
    scales = spread * rising
    diagonal = jnp.exp(jax.random.uniform(keys_all[3], (ORDER,), jnp.float32, 0.0, 2.3))
    row_noise = noise[row_global][:, col_global]
    col_noise = noise[col_global][:, row_global].T
    symmetric = (row_noise + col_noise) * 0.0707
    pair_scale = scales[row_global][:, None] * scales[col_global][None, :]
    on_diagonal = row_global[:, None] == col_global[None, :]
    result = symmetric * pair_scale + jnp.where(on_diagonal, diagonal[row_global][:, None], jnp.float32(0.0))
    return result


def setup_inputs(seed: int = 0) -> dict:
    keys = jax.random.split(jax.random.key(seed), 2)
    hamiltonian = draw_hamiltonian(jax.random.fold_in(keys[1], 71), 0)
    return {"hamiltonian": hamiltonian}


exact_mode = lax.Precision.HIGHEST

def product_of(left, right):
    return jnp.dot(left.astype(jnp.float32), right.astype(jnp.float32), precision=exact_mode, preferred_element_type=jnp.float32)

def inner_product(left, right):
    return lax.dot_general(left.astype(jnp.float32), right.astype(jnp.float32), (((0,), (0,)), ((), ())), precision=exact_mode, preferred_element_type=jnp.float32)

def outer_product(left, right):
    return lax.dot_general(left.astype(jnp.float32), right.astype(jnp.float32), (((1,), (1,)), ((), ())), precision=exact_mode, preferred_element_type=jnp.float32)

def lower_inverse(gram):
    lower = jnp.linalg.cholesky(gram)
    return jax.scipy.linalg.solve_triangular(lower, jnp.eye(gram.shape[0], dtype=jnp.float32), lower=True)

def reflector(panel, panel_index):
    row_start = (panel_index + 1) * NB
    global_index = jnp.arange(ORDER, dtype=jnp.int32)
    offsets = jnp.arange(NB, dtype=jnp.int32)
    panel = jnp.where((global_index >= row_start)[:, None], panel, jnp.float32(0.0))
    inverse_second = lower_inverse(inner_product(panel, panel))
    unit_rows = (global_index[:, None] == row_start + offsets[None, :]).astype(jnp.float32)
    vectors = outer_product(panel, inverse_second) + unit_rows
    top_block = outer_product(panel[row_start:row_start + NB], inverse_second)
    shifted = jnp.eye(NB, dtype=jnp.float32) + top_block
    factor = jnp.linalg.cholesky(inner_product(shifted, shifted))
    coupling = jax.scipy.linalg.cho_solve((factor, True), shifted.T).T
    return (vectors, coupling)

def reference(hamiltonian):
    prow_count = ORDER // ROWS_DEV
    pcol_count = ORDER // COLS_DEV
    stored = jnp.arange(ORDER, dtype=jnp.int32)
    row_global = (stored % ROWS_DEV // NB * prow_count + stored // ROWS_DEV) * NB + stored % NB
    col_global = (stored % COLS_DEV // NB * pcol_count + stored // COLS_DEV) * NB + stored % NB
    block_number = stored // NB
    row_stored = block_number % prow_count * ROWS_DEV + block_number // prow_count * NB + stored % NB
    col_stored = block_number % pcol_count * COLS_DEV + block_number // pcol_count * NB + stored % NB
    matrix = hamiltonian
    for panel_index in range(2):
        columns = col_stored[panel_index * NB:(panel_index + 1) * NB]
        panel = matrix[:, columns][row_stored]
        vectors, coupling = reflector(panel, panel_index)
        vector_rows = vectors[row_global]
        vector_cols = vectors[col_global]
        mixed = product_of(product_of(matrix, vector_cols), coupling)
        mixed_global = mixed[row_stored]
        folded = inner_product(vectors, mixed_global)
        correction = inner_product(coupling, folded)
        weights = mixed_global - 0.5 * product_of(vectors, correction)
        left_side = jnp.concatenate([vector_rows, weights[row_global]], axis=1)
        right_side = jnp.concatenate([weights[col_global], vector_cols], axis=1)
        matrix = matrix - outer_product(left_side, right_side)
    return matrix
```

```python
import functools

import jax
import jax.numpy as jnp
from jax import lax
from jax.experimental import pallas as pl
from jax.experimental.pallas import tpu as pltpu
from jax.sharding import PartitionSpec as P

NB = 128
PR = 16
PC = 32
NY = 8
NX = 4
CD = 512
SL = NB // PR

MESH = pl.DeviceIdType.MESH
exact_mode = lax.Precision.HIGHEST

SC_P, SC_E, B_P, B_E, G_P, G_E, RS, B_Y, G_Y, C_P, C_E, C_Y, A_RS, A_AG, Q_RS, Q_AG = range(16)


def dot_nn(a, b):
    return lax.dot_general(
        a, b, (((1,), (0,)), ((), ())), precision=exact_mode, preferred_element_type=jnp.float32
    )


def dot_nt(a, b):
    return lax.dot_general(
        a, b, (((1,), (1,)), ((), ())), precision=exact_mode, preferred_element_type=jnp.float32
    )


def dot_tn(a, b):
    return lax.dot_general(
        a, b, (((0,), (0,)), ((), ())), precision=exact_mode, preferred_element_type=jnp.float32
    )


def exchange_kernel(
    j,
    h_ref,
    pr,
    er,
    yr,
    pc,
    ec,
    yc,
    small,
    quad,
    part,
    rs_buf,
    ar_src,
    ar_buf,
    q_src,
    q_buf,
    send_sem,
    recv_sem,
):
    i = lax.axis_index("prow")
    k = lax.axis_index("pcol")
    y = k // NX
    x = k % NX
    half = x // 2
    f_mine = (x % 2) * NY + y
    k_mine = i + PR * half
    home = k_mine == k
    mine = pl.ds(pl.multiple_of(f_mine * SL, SL), SL)

    def holder(f):
        return (k % PR, NX * (f % NY) + 2 * (k // PR) + f // NY)

    def send(src, dst, which, target):
        pltpu.make_async_remote_copy(
            src_ref=src,
            dst_ref=dst,
            send_sem=send_sem.at[which],
            recv_sem=recv_sem.at[which],
            device_id=target,
            device_id_type=MESH,
        ).start()

    def send_or_copy(src, dst, which, target):
        same = jnp.logical_and(target[0] == i, target[1] == k)

        @pl.when(same)
        def _():
            pltpu.make_async_copy(src, dst, recv_sem.at[which]).start()

        @pl.when(jnp.logical_not(same))
        def _():
            send(src, dst, which, target)

    def loop(n, body):
        lax.fori_loop(0, n, lambda t, c: (body(t), c)[1], 0)

    def wait_recv(which, ref):
        pltpu.make_async_copy(ref, ref, recv_sem.at[which]).wait()

    def wait_send(which, ref):
        pltpu.make_async_copy(ref, ref, send_sem.at[which]).wait()

    barrier = pltpu.get_barrier_semaphore()

    def greet(target):
        same = jnp.logical_and(target[0] == i, target[1] == k)

        @pl.when(jnp.logical_not(same))
        def _():
            pl.semaphore_signal(barrier, inc=1, device_id=target, device_id_type=MESH)

    loop(PR, lambda t: greet(holder(t)))
    loop(PR, lambda t: greet((t, k_mine)))
    loop(NY - 1, lambda t: greet((i, NX * lax.rem(y + 1 + t, NY) + x)))
    loop(NX - 1, lambda t: greet((i, NX * y + lax.rem(x + 1 + t, NX))))
    loop(PR - 1, lambda t: greet((lax.rem(i + 1 + t, PR), k)))
    others = (NY - 1) + (NX - 1) + (PR - 1)

    @pl.when(home)
    def _():
        pl.semaphore_wait(barrier, others + 2 * (PR - 1))

    @pl.when(jnp.logical_not(home))
    def _():
        pl.semaphore_wait(barrier, others + 2 * PR)

    def scatter(dst, which):
        def body(t):
            rows = pl.ds(pl.multiple_of(t * SL, SL), SL)
            send_or_copy(h_ref.at[rows, :], dst.at[k // PR, rows, :], which, holder(t))

        loop(PR, body)

    def along_y(ref, which):
        def body(t):
            piece = ref.at[half, mine, :]
            send(piece, piece, which, (i, NX * lax.rem(y + 1 + t, NY) + x))

        loop(NY - 1, body)

    def along_x(ref, which):
        def body(t):
            run = ref.at[half, pl.ds(pl.multiple_of((x % 2) * (NB // 2), NB // 2), NB // 2), :]
            send(run, run, which, (i, NX * y + lax.rem(x + 1 + t, NX)))

        loop(NX - 1, body)

    def to_column(ref, dst, which):
        def body(t):
            send_or_copy(ref.at[half, mine, :], dst.at[mine, :], which, (t, k_mine))

        loop(PR, body)

    def got_y(ref, which):
        wait_recv(which, ref.at[0, pl.ds(0, (NY - 1) * SL), :])

    def got_x(ref, which):
        wait_recv(which, ref.at[:, pl.ds(0, 3 * NB // 4), :])

    @pl.when(i == j)
    def _():
        scatter(pr, SC_P)

    @pl.when(i == j + 1)
    def _():
        scatter(er, SC_E)

    wait_recv(SC_P, pr.at[half, mine, :])
    along_y(pr, B_P)
    wait_recv(SC_E, er.at[half, mine, :])
    along_y(er, B_E)
    got_y(pr, B_P)
    along_x(pr, G_P)
    to_column(pr, pc, C_P)
    got_x(pr, G_P)

    def panel_block(m):
        block = pr[m % 2, :, NB * (m // 2) : NB * (m // 2) + NB]
        if m == 0:
            block = jnp.where(i <= j, jnp.float32(0.0), block)
        return block

    product = dot_nn(panel_block(0), h_ref[0:NB, :])
    for m in range(1, 8):
        product += dot_nn(panel_block(m), h_ref[NB * m : NB * m + NB, :])
    part[...] = product

    def rs_body(t):
        rows = pl.ds(pl.multiple_of(t * SL, SL), SL)
        send_or_copy(part.at[rows, :], rs_buf.at[i], RS, holder(t))

    loop(PR, rs_body)

    gram = jnp.zeros((NB, NB), jnp.float32)
    for m in range(8):
        gram += dot_nt(panel_block(m), panel_block(m))
    ar_src[0] = gram

    got_y(er, B_E)
    along_x(er, G_E)
    to_column(er, ec, C_E)

    wait_recv(RS, rs_buf)
    total = rs_buf[0]
    for t in range(1, PR):
        total += rs_buf[t]
    yr[half, mine, :] = total
    along_y(yr, B_Y)
    to_column(yr, yc, C_Y)

    got_x(er, G_E)

    def cross(ref):
        total = jnp.zeros((NB, NB), jnp.float32)
        for m in range(8):
            total += dot_nt(
                panel_block(m), ref[m % 2, :, NB * (m // 2) : NB * (m // 2) + NB]
            )
        return total

    ar_src[1] = cross(er)
    ar_src[2] = jnp.where(i == j + 1, pr[0, :, 0:NB], jnp.float32(0.0))
    ar_src[3] = jnp.where(i == j + 1, er[0, :, 0:NB], jnp.float32(0.0))

    def ar_body(t):
        rows = pl.ds(pl.multiple_of(t * SL, SL), SL)
        send_or_copy(ar_src.at[:, rows, :], ar_buf.at[i], A_RS, (t, k))

    loop(PR, ar_body)

    got_y(yr, B_Y)
    along_x(yr, G_Y)

    own = pl.ds(pl.multiple_of(i * SL, SL), SL)
    wait_recv(A_RS, ar_buf)
    total = ar_buf[0]
    for t in range(1, PR):
        total += ar_buf[t]
    small[:, own, :] = total

    def ag_body(t):
        send(small.at[:, own, :], small.at[:, own, :], A_AG, (lax.rem(i + 1 + t, PR), k))

    loop(PR - 1, ag_body)

    got_x(yr, G_Y)
    q_src[...] = cross(yr)

    def q_body(t):
        rows = pl.ds(pl.multiple_of(t * SL, SL), SL)
        send_or_copy(q_src.at[rows, :], q_buf.at[i], Q_RS, (t, k))

    loop(PR, q_body)
    wait_recv(Q_RS, q_buf)
    total = q_buf[0]
    for t in range(1, PR):
        total += q_buf[t]
    quad[own, :] = total

    def qg_body(t):
        send(quad.at[own, :], quad.at[own, :], Q_AG, (lax.rem(i + 1 + t, PR), k))

    loop(PR - 1, qg_body)

    wait_recv(C_P, pc)
    wait_recv(C_E, ec)
    wait_recv(C_Y, yc)
    wait_recv(A_AG, small.at[:, pl.ds(0, NB - SL), :])
    wait_recv(Q_AG, quad.at[pl.ds(0, NB - SL), :])

    def sent_pieces(which):
        @pl.when(home)
        def _():
            wait_send(which, pr.at[0, pl.ds(0, NB - SL), :])

        @pl.when(jnp.logical_not(home))
        def _():
            wait_send(which, pr.at[0])

    @pl.when(i == j)
    def _():
        sent_pieces(SC_P)

    @pl.when(i == j + 1)
    def _():
        sent_pieces(SC_E)

    for which in (RS, C_P, C_E, C_Y):
        sent_pieces(which)
    for which in (B_P, B_E, B_Y):
        wait_send(which, pr.at[0, pl.ds(0, (NY - 1) * SL), :])
    for which in (G_P, G_E, G_Y):
        wait_send(which, pr.at[:, pl.ds(0, 3 * NB // 4), :])
    for which in (A_RS, A_AG):
        wait_send(which, small.at[:, pl.ds(0, NB - SL), :])
    for which in (Q_RS, Q_AG):
        wait_send(which, quad.at[pl.ds(0, NB - SL), :])


def exchange(j, matrix):
    f32 = jnp.float32
    vmem = pl.BlockSpec(memory_space=pltpu.VMEM)
    rows = jax.ShapeDtypeStruct((2, NB, CD), f32)
    cols = jax.ShapeDtypeStruct((NB, CD), f32)
    return pl.pallas_call(
        functools.partial(exchange_kernel, j),
        out_shape=(
            rows,
            rows,
            rows,
            cols,
            cols,
            cols,
            jax.ShapeDtypeStruct((4, NB, NB), f32),
            jax.ShapeDtypeStruct((NB, NB), f32),
        ),
        in_specs=[vmem],
        out_specs=(vmem,) * 8,
        scratch_shapes=[
            pltpu.VMEM((NB, CD), f32),
            pltpu.VMEM((PR, SL, CD), f32),
            pltpu.VMEM((4, NB, NB), f32),
            pltpu.VMEM((PR, 4, SL, NB), f32),
            pltpu.VMEM((NB, NB), f32),
            pltpu.VMEM((PR, SL, NB), f32),
            pltpu.SemaphoreType.DMA((16,)),
            pltpu.SemaphoreType.DMA((16,)),
        ],
        compiler_params=pltpu.CompilerParams(
            collective_id=j, has_side_effects=True, vmem_limit_bytes=32 * 1024 * 1024
        ),
        name=f"exchange_{j}",
    )(matrix)


def lower_inverse(gram):
    lower = jnp.linalg.cholesky(gram)
    return jax.scipy.linalg.solve_triangular(
        lower, jnp.eye(gram.shape[0], dtype=jnp.float32), lower=True
    )


def on_device(matrix):
    i = lax.axis_index("prow")
    k = lax.axis_index("pcol")
    eye = jnp.eye(NB, dtype=jnp.float32)
    first = (jnp.arange(CD) < NB)[None, :]
    unit = jnp.concatenate([eye, jnp.zeros((NB, CD - NB), jnp.float32)], axis=1)
    for j in range(2):
        pr, er, yr, pc, ec, yc, small, quad = exchange(j, matrix)
        gram, cross, top_t, corner = small[0], small[1], small[2], small[3]
        inverse_second = lower_inverse(gram)
        shifted = eye + dot_tn(top_t, inverse_second.T)
        factor = jnp.linalg.cholesky(dot_tn(shifted, shifted))
        coupling = jax.scipy.linalg.cho_solve((factor, True), shifted.T).T
        mixed = dot_nn(inverse_second, cross)
        inner = dot_nt(dot_nn(inverse_second, quad), inverse_second) + mixed + mixed.T + corner
        middle = dot_tn(coupling, dot_nn(inner, coupling))

        def factors(p, e, yv, index):
            p = jnp.where(jnp.logical_and(first, index <= j), jnp.float32(0.0), p)
            vectors = dot_nn(inverse_second, p)
            vectors += jnp.where(index == j + 1, unit, jnp.float32(0.0))
            image = dot_nn(inverse_second, yv) + e
            weights = dot_tn(coupling, image) - 0.5 * dot_tn(middle, vectors)
            return vectors, weights

        v0, w0 = factors(pr[0], er[0], yr[0], i)
        v1, w1 = factors(pr[1], er[1], yr[1], PR + k * 0)
        vc, wc = factors(pc, ec, yc, k)
        left = jnp.stack([jnp.concatenate([v0, w0]), jnp.concatenate([v1, w1])])
        left = left.reshape(2, 2 * NB, 4, NB).transpose(1, 2, 0, 3).reshape(2 * NB, 8 * NB)
        right = jnp.concatenate([wc, vc])
        matrix = matrix - dot_tn(left, right)
    return matrix


def solution(mesh):
    return jax.shard_map(
        on_device,
        mesh=mesh,
        in_specs=(P("prow", "pcol"),),
        out_specs=P("prow", "pcol"),
        check_vma=False,
    )
```

```python
import jax
import jax.numpy as jnp
from jax import lax
from jax.experimental import pallas as pl
from jax.experimental.pallas import tpu as pltpu
from jax.sharding import PartitionSpec as P

NB = 128
PR = 16
NZ = 8
NY = 8
NX = 4
CD = 512
SL = NB // PR
HF = NB // 2

MESH = pl.DeviceIdType.MESH
f32 = jnp.float32
exact_mode = lax.Precision.HIGHEST


def dot_nn(a, b):
    return lax.dot_general(
        a, b, (((1,), (0,)), ((), ())), precision=exact_mode, preferred_element_type=f32
    )


def dot_nt(a, b):
    return lax.dot_general(
        a, b, (((1,), (1,)), ((), ())), precision=exact_mode, preferred_element_type=f32
    )


def dot_tn(a, b):
    return lax.dot_general(
        a, b, (((0,), (0,)), ((), ())), precision=exact_mode, preferred_element_type=f32
    )


def eliminate(first, last, w_ref, g_ref, linv_ref, r_ref):
    lane = lax.broadcasted_iota(jnp.int32, (8, NB), 1)
    sub = lax.broadcasted_iota(jnp.int32, (8, NB), 0)
    zero = jnp.zeros((8, NB), f32)

    def body(b, carry):
        w, g = list(carry[:16]), list(carry[16:])
        left = NB - 8 * b
        scale = zero
        for s in range(8):
            here = lane == s
            row = jnp.broadcast_to(w[0][s : s + 1, :], (8, NB))
            d = jnp.broadcast_to(row[:, s : s + 1], (8, NB))
            rs = lax.rsqrt(d)
            scale = jnp.where(sub == s, rs, scale)
            rd = rs * rs
            step = jnp.where(here, rd, row * rd)
            grow = jnp.broadcast_to(g[0][s : s + 1, :], (8, NB))
            grow = grow + jnp.where(jnp.logical_and(lane >= s, lane < left), row * rs, 0.0)
            gd = 1.0 / jnp.broadcast_to(grow[:, s : s + 1], (8, NB))
            gstep = jnp.where(here, gd, grow * gd)
            for v in range(16):
                wc = jnp.broadcast_to(w[v][:, s : s + 1], (8, NB))
                gc = jnp.broadcast_to(g[v][:, s : s + 1], (8, NB))
                if v == 0:
                    w[0] = jnp.where(sub > s, jnp.where(here, 0.0, w[0]) - wc * step, w[0])
                    g[0] = jnp.where(sub == s, gstep, jnp.where(here, 0.0, g[0]) - gc * gstep)
                else:
                    w[v] = jnp.where(here, 0.0, w[v]) - wc * step
                    g[v] = jnp.where(here, 0.0, g[v]) - gc * gstep
        lower = jnp.logical_or(lane >= left, lane < sub)
        linv = scale * jnp.where(lower, w[0], jnp.where(lane == sub, 1.0, 0.0))
        upper = scale * jnp.where(lower, 0.0, w[0])
        rows = pl.ds(pl.multiple_of(8 * b, 8), 8)
        linv_ref[rows, :] = pltpu.roll(linv, 8 * b, 1)
        r_ref[rows, :] = pltpu.roll(upper, 8 * b, 1)
        w = [pltpu.roll(t, NB - 8, 1) for t in w[1:]] + [zero]
        g = [pltpu.roll(t, NB - 8, 1) for t in g[1:] + g[:1]]
        return tuple(w + g)

    init = tuple(w_ref[8 * v : 8 * v + 8, :] for v in range(16)) + tuple(
        g_ref[8 * v : 8 * v + 8, :] for v in range(16)
    )
    out = lax.fori_loop(first, last, body, init)
    for v in range(16):
        w_ref[8 * v : 8 * v + 8, :] = out[v]
        g_ref[8 * v : 8 * v + 8, :] = out[16 + v]


NAMES = (
    [a + b for a in ("P", "B", "C", "Y0", "Y1") for b in ("scatter", "y", "x", "turn", "z", "sib")]
    + [a + b for a in ("S", "Q0", "Q1") for b in ("sib", "z", "y", "x")]
    + [a + b for a in ("G0", "G1") for b in ("sib", "z", "back")]
)
NUMBER = {name: n for n, name in enumerate(NAMES)}


def kernel(
    h_ref,
    out_ref,
    xp,
    xb,
    xc,
    xy0,
    xy1,
    part0,
    part1,
    rs0,
    rs1,
    s_src,
    s_sib,
    s_z,
    s_gb,
    q0_src,
    q0_sib,
    q0_z,
    q0_gb,
    q1_src,
    q1_sib,
    q1_z,
    q1_gb,
    gsrc0,
    gsib0,
    gz0,
    gram0,
    gsrc1,
    gsib1,
    gz1,
    gram1,
    w_ref,
    g_ref,
    linv_ref,
    r_ref,
    vw,
    mid,
    send_sem,
    recv_sem,
):
    i = lax.axis_index("prow")
    k = lax.axis_index("pcol")
    y = k // NX
    x = k % NX
    z = i // 2
    core = i % 2
    sibling = (i + 1 - 2 * core, k)
    half = x // 2
    f_mine = (x % 2) * NY + y
    k_mine = i + PR * half
    home = k_mine == k
    mine = pl.ds(pl.multiple_of(f_mine * SL, SL), SL)
    turned = 2 * (f_mine % NZ) + f_mine // NZ
    turn_home = jnp.logical_and(home, turned == i)
    z_rows = pl.ds(pl.multiple_of((core * NZ + z) * SL, SL), SL)
    core_rows = pl.ds(pl.multiple_of(core * HF, HF), HF)
    other_rows = pl.ds(pl.multiple_of(HF - core * HF, HF), HF)

    def holder(f):
        return (k % PR, NX * (f % NY) + 2 * (k // PR) + f // NY)

    def y_mate(t):
        return (i, NX * lax.rem(y + 1 + t, NY) + x)

    def x_mate(t):
        return (i, NX * y + lax.rem(x + 1 + t, NX))

    def z_mate(t):
        return (lax.rem(i + 2 + 2 * t, PR), k)

    def send(src, dst, name, target):
        n = NUMBER[name]
        pltpu.make_async_remote_copy(
            src_ref=src,
            dst_ref=dst,
            send_sem=send_sem.at[n],
            recv_sem=recv_sem.at[n],
            device_id=target,
            device_id_type=MESH,
        ).start()

    def send_or_copy(src, dst, name, target):
        same = jnp.logical_and(target[0] == i, target[1] == k)

        @pl.when(same)
        def _():
            pltpu.make_async_copy(src, dst, recv_sem.at[NUMBER[name]]).start()

        @pl.when(jnp.logical_not(same))
        def _():
            send(src, dst, name, target)

    def loop(n, body):
        lax.fori_loop(0, n, lambda t, c: (body(t), c)[1], 0)

    def got(name, ref):
        pltpu.make_async_copy(ref, ref, recv_sem.at[NUMBER[name]]).wait()

    def sent(name, ref):
        pltpu.make_async_copy(ref, ref, send_sem.at[NUMBER[name]]).wait()

    def when(condition, body):
        @pl.when(condition)
        def _():
            body()

    barrier = pltpu.get_barrier_semaphore()

    def greet(target):
        same = jnp.logical_and(target[0] == i, target[1] == k)

        @pl.when(jnp.logical_not(same))
        def _():
            pl.semaphore_signal(barrier, inc=1, device_id=target, device_id_type=MESH)

    loop(PR, lambda t: greet(holder(t)))
    loop(PR, lambda t: greet((t, k_mine)))
    loop(NY - 1, lambda t: greet(y_mate(t)))
    loop(NX - 1, lambda t: greet(x_mate(t)))
    loop(NZ - 1, lambda t: greet(z_mate(t)))
    greet(sibling)
    others = (NY - 1) + (NX - 1) + (NZ - 1) + 1
    when(home, lambda: pl.semaphore_wait(barrier, others + 2 * (PR - 1)))
    when(jnp.logical_not(home), lambda: pl.semaphore_wait(barrier, others + 2 * PR))


    def scatter(ref, name):
        def body(t):
            rows = pl.ds(pl.multiple_of(t * SL, SL), SL)
            send_or_copy(h_ref.at[rows, :], ref.at[k // PR, rows, :], name + "scatter", holder(t))

        loop(PR, body)

    def along_y(ref, name):
        piece = ref.at[half, mine, :]
        loop(NY - 1, lambda t: send(piece, piece, name + "y", y_mate(t)))

    def along_x(ref, name):
        got(name + "y", ref.at[0, pl.ds(0, (NY - 1) * SL), :])
        run = ref.at[half, pl.ds(pl.multiple_of((x % 2) * HF, HF), HF), :]
        loop(NX - 1, lambda t: send(run, run, name + "x", x_mate(t)))

    def got_row(ref, name):
        got(name + "x", ref.at[pl.ds(0, 2), pl.ds(0, 3 * NB // 4), :])

    def turn(ref, name):
        send_or_copy(ref.at[half, mine, :], ref.at[2, mine, :], name + "turn", (turned, k_mine))

    def along_z(ref, name):
        piece = ref.at[2, z_rows, :]
        got(name + "turn", piece)
        loop(NZ - 1, lambda t: send(piece, piece, name + "z", z_mate(t)))

    def to_sibling(ref, name):
        got(name + "z", ref.at[2, pl.ds(0, (NZ - 1) * SL), :])
        run = ref.at[2, core_rows, :]
        send(run, run, name + "sib", sibling)

    def got_column(ref, name):
        got(name + "sib", ref.at[2, pl.ds(0, HF), :])


    def flow_start(name, src, sib):
        send(src, sib, name + "sib", sibling)

    def flow_z(name, src, sib, zb):
        got(name + "sib", sib)
        zb[z] = src[...] + sib[...]
        loop(NZ - 1, lambda t: send(zb.at[z], zb.at[z], name + "z", z_mate(t)))

    def flow_y(name, zb, gb):
        got(name + "z", zb.at[pl.ds(0, NZ - 1)])
        total = zb[0]
        for t in range(1, NZ):
            total += zb[t]
        rows = pl.ds(pl.multiple_of(y * SL, SL), SL)
        gb[x, rows, :] = total
        piece = gb.at[x, rows, :]
        loop(NY - 1, lambda t: send(piece, piece, name + "y", y_mate(t)))

    def flow_x(name, gb):
        got(name + "y", gb.at[0, pl.ds(0, (NY - 1) * SL), :])
        loop(NX - 1, lambda t: send(gb.at[x], gb.at[x], name + "x", x_mate(t)))

    def flow_end(name, gb):
        got(name + "x", gb.at[pl.ds(0, NX - 1)])

    def block(gb, n):
        lanes = slice(NB * n, NB * n + NB)
        return jnp.concatenate(
            [gb[0, :, lanes] + gb[2, :, lanes], gb[1, :, lanes] + gb[3, :, lanes]], axis=0
        )


    def gram_start(name, src, sib):
        send(src.at[other_rows, :], sib, name + "sib", sibling)

    def gram_z(name, src, sib, zb):
        got(name + "sib", sib)
        zb[z] = src[core_rows, :] + sib[...]
        loop(NZ - 1, lambda t: send(zb.at[z], zb.at[z], name + "z", z_mate(t)))

    def gram_back(name, zb, dst):
        got(name + "z", zb.at[pl.ds(0, NZ - 1)])
        total = zb[0]
        for t in range(1, NZ):
            total += zb[t]
        dst[core_rows, :] = total
        send(dst.at[core_rows, :], dst.at[core_rows, :], name + "back", sibling)

    def gram_end(name, dst):
        got(name + "back", dst.at[pl.ds(0, HF), :])

    def masked(value, index, j):
        lane = lax.broadcasted_iota(jnp.int32, value.shape, 1)
        return jnp.where(jnp.logical_and(lane < NB, index <= j), 0.0, value)

    def own_block(value, row):
        return jnp.where(jnp.logical_and(half == 0, i == row), value, 0.0)

    def reduce_scatter(part, buf, name):
        def body(t):
            rows = pl.ds(pl.multiple_of(t * SL, SL), SL)
            send_or_copy(part.at[rows, :], buf.at[i], name, holder(t))

        loop(PR, body)

    def times_matrix(rows):
        total = jnp.zeros((NB, CD), f32)
        for h in range(2):
            for m in range(4):
                lb = 2 * m + h
                total += dot_nn(rows[h][:, NB * m : NB * m + NB], h_ref[NB * lb : NB * lb + NB, :])
        return total

    def add_up(buf):
        total = buf[0]
        for t in range(1, PR):
            total += buf[t]
        return total

    when(i == 0, lambda: scatter(xp, "P"))
    when(i == 1, lambda: scatter(xb, "B"))
    when(i == 2, lambda: scatter(xc, "C"))

    got("Pscatter", xp.at[half, mine, :])
    along_y(xp, "P")
    turn(xp, "P")
    got("Bscatter", xb.at[half, mine, :])
    along_y(xb, "B")
    turn(xb, "B")
    got("Cscatter", xc.at[half, mine, :])
    along_y(xc, "C")
    turn(xc, "C")
    blocks = [(xp, 1), (xp, 2), (xb, 1), (xb, 2), (xc, 2)]
    for n, (ref, row) in enumerate(blocks):
        s_src[:, NB * n : NB * n + NB] = own_block(ref[half, mine, 0:NB], row)
    flow_start("S", s_src, s_sib)
    along_x(xp, "P")
    flow_z("S", s_src, s_sib, s_z)
    along_z(xp, "P")
    along_x(xb, "B")
    along_x(xc, "C")
    got_row(xp, "P")

    panel = [masked(xp[0], i, 0), xp[1]]
    part0[...] = times_matrix(panel)
    reduce_scatter(part0, rs0, "Y0scatter")
    gsrc0[...] = dot_nt(panel[0], panel[0]) + dot_nt(panel[1], panel[1])
    gram_start("G0", gsrc0, gsib0)
    flow_y("S", s_z, s_gb)
    along_z(xb, "B")
    along_z(xc, "C")
    gram_z("G0", gsrc0, gsib0, gz0)
    to_sibling(xp, "P")

    def image_pieces(rs, ref, name, j, q_src, rows):
        got(name + "scatter", rs)
        piece = add_up(rs)
        ref[half, mine, :] = piece
        along_y(ref, name)
        turn(ref, name)
        panel_half = jnp.where(half == 0, rows[0], rows[1])
        q_src[:, 0:NB] = dot_nt(piece, panel_half)
        for n, row in enumerate(range(j + 1, 3)):
            q_src[:, NB * (n + 1) : NB * (n + 2)] = own_block(piece[:, 0:NB], row)

    image_pieces(rs0, xy0, "Y0", 0, q0_src, panel)
    flow_start("Q0", q0_src, q0_sib)
    flow_x("S", s_gb)
    gram_back("G0", gz0, gram0)
    flow_z("Q0", q0_src, q0_sib, q0_z)
    along_x(xy0, "Y0")
    along_z(xy0, "Y0")
    gram_end("G0", gram0)
    flow_end("S", s_gb)

    w_ref[...] = gram0[...]
    g_ref[...] = block(s_gb, 0).T
    eliminate(0, 3, w_ref, g_ref, linv_ref, r_ref)
    flow_y("Q0", q0_z, q0_gb)
    eliminate(3, 8, w_ref, g_ref, linv_ref, r_ref)
    flow_x("Q0", q0_gb)
    to_sibling(xb, "B")
    to_sibling(xc, "C")
    to_sibling(xy0, "Y0")
    eliminate(8, 16, w_ref, g_ref, linv_ref, r_ref)

    def middle(quad, cross, corner):
        linv = linv_ref[...]
        coupling_t = dot_nn(r_ref[...], g_ref[...])
        mid[0] = dot_nn(linv, cross)
        mid[1] = dot_nt(dot_nn(linv, quad), linv)
        mid[2] = mid[0].T
        mid[3] = mid[1] + mid[0] + mid[2] + corner
        inner = dot_nt(dot_nn(coupling_t, mid[3]), coupling_t)
        return linv, coupling_t, inner

    def factors(mats, p, unit, image, e):
        linv, coupling_t, inner = mats
        vectors = dot_nn(linv, p) + unit
        weights = dot_nn(coupling_t, dot_nn(linv, image) + e) - 0.5 * dot_nn(inner, vectors)
        return vectors, weights

    def unit_at(condition, width):
        lane = lax.broadcasted_iota(jnp.int32, (NB, width), 1)
        row = lax.broadcasted_iota(jnp.int32, (NB, width), 0)
        return jnp.where(jnp.logical_and(lane == row, condition), 1.0, 0.0)

    flow_end("Q0", q0_gb)
    p_b = jnp.concatenate([block(s_gb, 0), block(s_gb, 1)], axis=1)
    b_b = jnp.concatenate([block(s_gb, 2), block(s_gb, 3)], axis=1)
    c_b2 = block(s_gb, 4)
    y_b = jnp.concatenate([block(q0_gb, 1), block(q0_gb, 2)], axis=1)
    mats = middle(block(q0_gb, 0), y_b[:, 0:NB], b_b[:, 0:NB])
    v_b, w_b = factors(mats, p_b, unit_at(True, 2 * NB), y_b, b_b)
    v_1, w_1 = v_b[:, 0:NB], w_b[:, 0:NB]
    v_2, w_2 = v_b[:, NB:], w_b[:, NB:]
    top1 = b_b[:, NB:] - dot_tn(w_1, v_2) - dot_tn(v_1, w_2)
    corner1 = c_b2 - dot_tn(w_2, v_2) - dot_tn(v_2, w_2)

    got_row(xb, "B")
    got_row(xy0, "Y0")
    got_row(xc, "C")
    for name, ref in (("P", xp), ("B", xb), ("C", xc), ("Y0", xy0)):
        got_column(ref, name)
    index = (i, PR, k)
    for s in range(3):
        p = xp[s] if s == 1 else masked(xp[s], index[s], 0)
        unit = 0.0 if s == 1 else unit_at(index[s] == 1, CD)
        v, w = factors(mats, p, unit, xy0[s], xb[s])
        vw[s, 0:NB, :] = v
        vw[s, NB : 2 * NB, :] = w

    next_panel, next_block = [], []
    for s in range(3):
        v, w = vw[s, 0:NB, :], vw[s, NB : 2 * NB, :]
        p = xb[s] - dot_tn(w_1, v) - dot_tn(v_1, w)
        next_panel.append(p if s == 1 else masked(p, index[s], 1))
        next_block.append(xc[s] - dot_tn(w_2, v) - dot_tn(v_2, w))

    rows = next_panel[0:2]
    across = dot_nt(rows[0], vw[0, 0 : 2 * NB, :]) + dot_nt(rows[1], vw[1, 0 : 2 * NB, :])
    part1[...] = (
        times_matrix(rows)
        - dot_nn(across[:, 0:NB], vw[2, NB : 2 * NB, :])
        - dot_nn(across[:, NB:], vw[2, 0:NB, :])
    )
    reduce_scatter(part1, rs1, "Y1scatter")
    gsrc1[...] = dot_nt(rows[0], rows[0]) + dot_nt(rows[1], rows[1])
    gram_start("G1", gsrc1, gsib1)
    gram_z("G1", gsrc1, gsib1, gz1)
    image_pieces(rs1, xy1, "Y1", 1, q1_src, rows)
    flow_start("Q1", q1_src, q1_sib)
    gram_back("G1", gz1, gram1)
    flow_z("Q1", q1_src, q1_sib, q1_z)
    along_x(xy1, "Y1")
    along_z(xy1, "Y1")
    gram_end("G1", gram1)
    w_ref[...] = gram1[...]
    g_ref[...] = top1.T
    eliminate(0, 3, w_ref, g_ref, linv_ref, r_ref)
    flow_y("Q1", q1_z, q1_gb)
    eliminate(3, 8, w_ref, g_ref, linv_ref, r_ref)
    flow_x("Q1", q1_gb)
    to_sibling(xy1, "Y1")
    eliminate(8, 16, w_ref, g_ref, linv_ref, r_ref)
    flow_end("Q1", q1_gb)
    mats = middle(block(q1_gb, 0), block(q1_gb, 1), corner1)
    got_row(xy1, "Y1")
    got_column(xy1, "Y1")
    for s in range(3):
        unit = 0.0 if s == 1 else unit_at(index[s] == 2, CD)
        v, w = factors(mats, next_panel[s], unit, xy1[s], next_block[s])
        vw[s, 2 * NB : 3 * NB, :] = v
        vw[s, 3 * NB : 4 * NB, :] = w

    right = jnp.concatenate(
        [vw[2, NB * n : NB * n + NB, :] for n in (1, 0, 3, 2)], axis=0
    )
    for h in range(2):
        for m in range(4):
            lb = NB * (2 * m + h)
            update = dot_tn(vw[h, :, NB * m : NB * m + NB], right)
            out_ref[lb : lb + NB, :] = h_ref[lb : lb + NB, :] - update

    def sent_pieces(name):
        when(home, lambda: sent(name, xp.at[0, pl.ds(0, NB - SL), :]))
        when(jnp.logical_not(home), lambda: sent(name, xp.at[0]))

    when(i == 0, lambda: sent_pieces("Pscatter"))
    when(i == 1, lambda: sent_pieces("Bscatter"))
    when(i == 2, lambda: sent_pieces("Cscatter"))
    sent_pieces("Y0scatter")
    sent_pieces("Y1scatter")
    for name in ("P", "B", "C", "Y0", "Y1"):
        sent(name + "y", xp.at[0, pl.ds(0, (NY - 1) * SL), :])
        sent(name + "x", xp.at[pl.ds(0, 2), pl.ds(0, 3 * NB // 4), :])
        when(
            jnp.logical_not(turn_home),
            lambda name=name: sent(name + "turn", xp.at[0, pl.ds(0, SL), :]),
        )
        sent(name + "z", xp.at[0, pl.ds(0, (NZ - 1) * SL), :])
        sent(name + "sib", xp.at[0, pl.ds(0, HF), :])
    for name, sib, zb, gb in (
        ("S", s_sib, s_z, s_gb),
        ("Q0", q0_sib, q0_z, q0_gb),
        ("Q1", q1_sib, q1_z, q1_gb),
    ):
        sent(name + "sib", sib)
        sent(name + "z", zb.at[pl.ds(0, NZ - 1)])
        sent(name + "y", gb.at[0, pl.ds(0, (NY - 1) * SL), :])
        sent(name + "x", gb.at[pl.ds(0, NX - 1)])
    for name, sib, zb, dst in (("G0", gsib0, gz0, gram0), ("G1", gsib1, gz1, gram1)):
        sent(name + "sib", sib)
        sent(name + "z", zb.at[pl.ds(0, NZ - 1)])
        sent(name + "back", dst.at[pl.ds(0, HF), :])


def on_device(matrix):
    vmem = pl.BlockSpec(memory_space=pltpu.VMEM)

    def flow(width):
        return [
            pltpu.VMEM((SL, width), f32),
            pltpu.VMEM((SL, width), f32),
            pltpu.VMEM((NZ, SL, width), f32),
            pltpu.VMEM((NX, HF, width), f32),
        ]

    def gram():
        return [
            pltpu.VMEM((NB, NB), f32),
            pltpu.VMEM((HF, NB), f32),
            pltpu.VMEM((NZ, HF, NB), f32),
            pltpu.VMEM((NB, NB), f32),
        ]

    return pl.pallas_call(
        kernel,
        out_shape=jax.ShapeDtypeStruct(matrix.shape, f32),
        in_specs=[vmem],
        out_specs=vmem,
        scratch_shapes=(
            [pltpu.VMEM((3, NB, CD), f32)] * 5
            + [pltpu.VMEM((NB, CD), f32)] * 2
            + [pltpu.VMEM((PR, SL, CD), f32)] * 2
            + flow(5 * NB)
            + flow(3 * NB)
            + flow(2 * NB)
            + gram()
            + gram()
            + [pltpu.VMEM((NB, NB), f32)] * 4
            + [pltpu.VMEM((3, 4 * NB, CD), f32), pltpu.VMEM((4, NB, NB), f32)]
            + [pltpu.SemaphoreType.DMA((len(NAMES),))] * 2
        ),
        compiler_params=pltpu.CompilerParams(
            collective_id=0, has_side_effects=True, vmem_limit_bytes=48 * 1024 * 1024
        ),
        name="band_reduction",
    )(matrix)


def solution(mesh):
    return jax.shard_map(
        on_device,
        mesh=mesh,
        in_specs=(P("prow", "pcol"),),
        out_specs=P("prow", "pcol"),
        check_vma=False,
    )
```
